256 devices in a mesh: row: 8 (over x, core), col: 8 (over y, z_hi), band: 4 (over z_lo).
Axes of the slice: x: 4, y: 4, z: 8 (z_hi: 2, z_lo: 4; z = z_hi * 4 + z_lo), core: 2. Of those that a mesh axis runs over, the one named last changes fastest.
Arguments:
- frames: bfloat16 [512, 128, 2, 1024], P(('row', 'col'), 'band'), may hold values from -6 to 6
- tail_frames: bfloat16 [512, 15, 2, 1024], P(('row', 'col')), may hold values from -6 to 6
- prototype: float32 [16, 1024], replicated, may hold values from -1.5 to 1.5
Outputs:
- visibility: float32 [512, 8, 64, 2, 1024], P('row', 'col', None, None, 'band')
The draws below stay inside these ranges and needn't reach their ends.
All inputs are finite; a program needn't handle non-finite values.
Results may differ from the reference program's by a relative error of at most 0.0059.
Values may be sent and summed in bfloat16 or wider, within the bound.
No kernel may reach another device: no remote copies, remote signals or barrier semaphores. Data moves between devices by JAX's collectives and lax.ppermute only.
A program may use at most 128 MiB of HBM per device.

```python
import math
import jax
import jax.numpy as jnp
from jax import lax

CHANNELS = 1024
TAPS = 16
INPUTS = 512
SPECTRA = 128
N_ROW = 8
N_COL = 8


def block_scale(own_key, extent, split, least, high):
    loudness = 1.0
    for position, shards_of in split:
        steps = jax.random.uniform(jax.random.fold_in(jax.random.fold_in(own_key, 6), position), (shards_of,), jnp.float32, least / len(split), high / len(split))
        loudness = loudness * jnp.repeat(jnp.exp(steps), extent[position] // shards_of).reshape((-1,) + (1,) * (len(extent) - 1 - position))
    return loudness


def noise(stream_key, extent, deviation, reach, cuts=(), held_as=jnp.bfloat16):
    values = deviation * jax.random.normal(stream_key, extent, jnp.float32)
    if cuts:
        values = values * block_scale(stream_key, extent, cuts, -0.22, 0.18)
    return jnp.clip(values, -reach, reach).astype(held_as)


def setup_inputs(seed: int = 0) -> dict:
    seeds = jax.random.split(jax.random.key(seed), 4)
    return {
        "frames": noise(seeds[0], (INPUTS, SPECTRA, 2, CHANNELS), 1.0, 6.0, ((0, 64), (1, 4))),
        "tail_frames": noise(seeds[1], (INPUTS, TAPS - 1, 2, CHANNELS), 1.0, 6.0, ((0, 64),)),
        "prototype": noise(seeds[2], (TAPS, CHANNELS), TAPS ** -0.5, 1.5, (), jnp.float32),
    }


def dft_table(n_chan, output_part):
    sample = jnp.arange(n_chan, dtype=jnp.int32)[:, None]
    channel = jnp.arange(n_chan, dtype=jnp.int32)[None, :]
    theta = 2.0 * math.pi / n_chan * (sample * channel % n_chan).astype(jnp.float32)
    cosine = jnp.cos(theta)
    sine = jnp.sin(theta)
    if output_part == 0:
        return jnp.concatenate([cosine, sine], 0).astype(jnp.bfloat16)
    return jnp.concatenate([-sine, cosine], 0).astype(jnp.bfloat16)

def reference(frames, tail_frames, prototype):
    extended = jnp.concatenate([frames, tail_frames], 1)
    summed = jnp.zeros(frames.shape, jnp.float32)
    for tap in range(TAPS):
        summed = summed + prototype[tap][None, None, None, :] * extended[:, tap:tap + SPECTRA].astype(jnp.float32)
    filtered = summed.astype(jnp.bfloat16).reshape(INPUTS * SPECTRA, 2 * CHANNELS)
    table = jnp.concatenate([dft_table(CHANNELS, 0), dft_table(CHANNELS, 1)], 1)
    spectra = jnp.dot(filtered, table, preferred_element_type=jnp.float32) * (1.0 / math.sqrt(CHANNELS))
    spectra = spectra.astype(jnp.bfloat16).reshape(INPUTS, SPECTRA, 2, CHANNELS)
    group_inputs = INPUTS // (N_ROW * N_COL)
    columns = spectra.reshape(N_ROW, N_COL, group_inputs, SPECTRA, 2, CHANNELS)
    columns = columns.transpose(1, 0, 2, 3, 4, 5).reshape(INPUTS, SPECTRA, 2, CHANNELS)
    width = 64 if CHANNELS % 64 == 0 else CHANNELS
    blocks = CHANNELS // width
    left_blocks = spectra.reshape(INPUTS, SPECTRA, 2, blocks, width).transpose(3, 0, 1, 2, 4)
    right_blocks = columns.reshape(INPUTS, SPECTRA, 2, blocks, width).transpose(3, 0, 1, 2, 4)

    def correlate(pair):
        left_part = pair[0].astype(jnp.float32)
        right_part = pair[1].astype(jnp.float32)
        outer = jnp.einsum('ascn,bsdn->abcdn', left_part, right_part)
        real_part = outer[:, :, 0, 0] + outer[:, :, 1, 1]
        imag_part = outer[:, :, 1, 0] - outer[:, :, 0, 1]
        return jnp.stack([real_part, imag_part], 2) * (1.0 / SPECTRA)
    result = lax.map(correlate, (left_blocks, right_blocks))
    result = result.transpose(1, 2, 3, 0, 4).reshape(INPUTS, INPUTS, 2, CHANNELS)
    return result.reshape(INPUTS, N_COL, N_ROW * group_inputs, 2, CHANNELS)
```

```python
import functools
import math

import jax
import jax.numpy as jnp
import numpy as np
from jax import lax
from jax.experimental import pallas as pl
from jax.experimental.pallas import tpu as pltpu
from jax.sharding import Mesh
from jax.sharding import PartitionSpec as P

LANES = 128
TAPS = 16
HALF = 16
INPUTS = 8
BANDS = 4
CHAN = 1024
VMEM_LIMIT = 48 * 1024 * 1024


def dft_table():
    sample = np.arange(CHAN, dtype=np.int64)[:, None]
    channel = np.arange(CHAN, dtype=np.int64)[None, :]
    theta = np.float32(2.0 * math.pi / CHAN) * (sample * channel % CHAN).astype(np.float32)
    parts = []
    for trig in (np.cos, np.sin):
        full = trig(theta.astype(np.float64)).astype(np.float32)
        parts.append(full.reshape(CHAN, BANDS, 2, LANES))
    table = np.stack(parts)
    table = table.transpose(3, 1, 0, 2, 4).reshape(2, CHAN, 2 * BANDS * LANES)
    return jnp.asarray(table, dtype=jnp.bfloat16)


def filter_transform_kernel(late, *refs):
    if late:
        flag_ref, first_ref, recv_ref, tail_ref, coeff_ref, table_ref, out0, out1, sums, lhs = refs
    else:
        first_ref, coeff_ref, table_ref, out0, out1, sums, lhs = refs
    tiles = CHAN // LANES

    def frame(a, t):
        if t < HALF:
            return first_ref[a, t].astype(jnp.float32)
        if not late:
            return first_ref[a, t].astype(jnp.float32)
        t -= HALF
        last = flag_ref[0] == 1
        return jnp.where(last, tail_ref[a, t], recv_ref[a, t]).astype(jnp.float32)

    def one_input(a, carry):
        acc = [None] * HALF
        for t in range(HALF + TAPS - 1):
            value = frame(a, t)
            for s in range(max(0, t - TAPS + 1), min(HALF, t + 1)):
                term = coeff_ref[t - s] * value
                acc[s] = term if acc[s] is None else acc[s] + term
        for s in range(HALF):
            sums[pl.ds(s * 16, 16), :] = acc[s]
        for k in range(tiles):
            for c in range(2):
                rows = sums[pl.ds(2 * k + c, HALF, 16), :]
                start = pl.multiple_of((a * 2 + c) * HALF, HALF)
                lhs[pl.ds(start, HALF), k * LANES : (k + 1) * LANES] = rows.astype(jnp.bfloat16)
        return carry

    lax.fori_loop(0, INPUTS, one_input, 0)
    scale = 1.0 / math.sqrt(CHAN)
    width = BANDS * LANES
    for half, out in enumerate((out0, out1)):
        both = jnp.dot(lhs[...], table_ref[half], preferred_element_type=jnp.float32)
        both = both.reshape(INPUTS, 2, HALF, 2 * width)
        real = (both[:, 0, :, :width] + both[:, 1, :, width:]) * scale
        imag = (both[:, 1, :, :width] - both[:, 0, :, width:]) * scale
        for band in range(BANDS):
            cols = slice(band * LANES, (band + 1) * LANES)
            for part, value in enumerate((real, imag)):
                value = value[:, :, cols].astype(jnp.bfloat16)
                out[band, :, part] = value
                out[band + BANDS, :, part] = value


def filter_transform(late, coeff, table, first, recv=None, tail=None, flag=None):
    block = jax.ShapeDtypeStruct((2 * BANDS, INPUTS, 2, HALF, LANES), jnp.bfloat16)
    vmem = pl.BlockSpec(memory_space=pltpu.VMEM)
    if late:
        args = (flag, first, recv, tail, coeff, table)
        in_specs = [pl.BlockSpec(memory_space=pltpu.SMEM)]
        in_specs += [pl.BlockSpec((INPUTS, HALF, 16, LANES), lambda i: (0, 1, 0, 0))]
        in_specs += [vmem] * 4
    else:
        args = (first, coeff, table)
        in_specs = [vmem] * 3
    return pl.pallas_call(
        functools.partial(filter_transform_kernel, late),
        out_shape=(block, block),
        grid=(1,),
        in_specs=in_specs,
        out_specs=(vmem, vmem),
        scratch_shapes=[
            pltpu.VMEM((HALF * 16, LANES), jnp.float32),
            pltpu.VMEM((INPUTS * 2 * HALF, CHAN), jnp.bfloat16),
        ],
        compiler_params=pltpu.CompilerParams(vmem_limit_bytes=VMEM_LIMIT),
        cost_estimate=pl.CostEstimate(
            flops=2 * 2 * 256 * CHAN * CHAN, bytes_accessed=8 << 20, transcendentals=0
        ),
        name="filter_transform",
    )(*args)


def turn_kernel(group_ref, recv_ref, out_ref, own_ref, rows):
    for high in range(2):
        for a in range(INPUTS):
            pieces = [recv_ref[high * BANDS + low, a, c] for c in range(2) for low in range(BANDS)]
            block = jnp.concatenate(pieces, 0).astype(jnp.float32)
            rows[pl.ds(high * INPUTS + a, LANES, 16), :] = block.T
    start = pl.multiple_of(group_ref[0] * INPUTS, INPUTS)

    def one(n, carry):
        base = pl.multiple_of(n * 16, 16)
        out_ref[n] = rows[pl.ds(base, 16), :].astype(jnp.bfloat16)
        mine = pl.multiple_of(base + start, 8)
        own_ref[n] = rows[pl.ds(mine, INPUTS), :].astype(jnp.bfloat16)
        return carry

    lax.fori_loop(0, LANES, one, 0, unroll=8)


def turn(group, recv):
    vmem = pl.BlockSpec(memory_space=pltpu.VMEM)
    return pl.pallas_call(
        turn_kernel,
        out_shape=(
            jax.ShapeDtypeStruct((LANES, 2 * INPUTS, LANES), jnp.bfloat16),
            jax.ShapeDtypeStruct((LANES, INPUTS, LANES), jnp.bfloat16),
        ),
        in_specs=[pl.BlockSpec(memory_space=pltpu.SMEM), vmem],
        out_specs=(vmem, vmem),
        scratch_shapes=[pltpu.VMEM((LANES * 16, LANES), jnp.float32)],
        compiler_params=pltpu.CompilerParams(vmem_limit_bytes=VMEM_LIMIT),
        cost_estimate=pl.CostEstimate(flops=1 << 20, bytes_accessed=2 << 20, transcendentals=0),
        name="turn",
    )(group, recv)


ROWS = 64
N_PIECE = 11


def correlate_kernel(half, spectra, place_ref, *refs):
    early, late = refs[:N_PIECE], refs[N_PIECE : 2 * N_PIECE]
    out_ref, outer, mixed = refs[-3:]
    step = pl.program_id(0)
    sign = jnp.where(lax.broadcasted_iota(jnp.int32, (ROWS, LANES), 1) < LANES // 2, -1.0, 1.0)

    first_core = place_ref[9] == 0

    def multiply(second, n):
        m = n + second * (LANES // 2)
        left, right = [], []
        for own, below, above, far0, far1, own8, sib8, got, got2, swap, swap2 in (early, late):
            far = far1 if second else far0
            left.append(jnp.concatenate([own[m], above[m], far[n], below[m]], 0))
            pieces = [own8[m], sib8[m], got[0, m], got[1, m], swap[0, m], swap[1, m]]
            came, other = (swap2, got2) if second else (got2, swap2)
            for i in (1, 0) if second else (0, 1):
                pieces.append(jnp.where(first_core, came[i, n], other[i, n]))
            right.append(jnp.concatenate([p.astype(jnp.float32) for p in pieces], 0))
        lhs = jnp.concatenate(left, 1)
        turned = [pltpu.roll(r, LANES // 2, 1) * sign for r in right]
        rhs = jnp.concatenate([jnp.concatenate(right, 1), jnp.concatenate(turned, 1)], 0)
        value = lax.dot_general(
            lhs,
            rhs.astype(jnp.bfloat16),
            (((1,), (1,)), ((), ())),
            preferred_element_type=jnp.float32,
        )
        outer[pl.ds(pl.multiple_of(m * ROWS, ROWS), ROWS), :] = value

    @pl.when(step == 0)
    def _():
        for second in range(2):

            def one(n, carry):
                multiply(second, n)
                return carry

            lax.fori_loop(0, LANES // 2, one, 0, unroll=4)

    my_y = place_ref[0]
    slot = lax.rem(step - my_y + 4, 4)

    def write(i, carry):
        column = slot * 16 + i
        block = outer[pl.ds(column, LANES, ROWS), :].T * (1.0 / spectra)
        for r in range(8):
            target = place_ref[1 + r] * 16
            for part in range(2):
                mixed[pl.ds(target + part, 8, 2), :] = block[part * 64 + r * 8 : part * 64 + r * 8 + 8]
        out_ref[i, 0] = mixed[...].reshape(ROWS, 2, LANES)
        return carry

    lax.fori_loop(0, 16, write, 0, unroll=2)


def correlate(half, spectra, place, early, late, previous):
    vmem = pl.BlockSpec(memory_space=pltpu.VMEM)
    smem = pl.BlockSpec(memory_space=pltpu.SMEM)
    extra, aliases = (), {}
    kernel = functools.partial(correlate_kernel, half, spectra)
    if previous is not None:
        extra, aliases = (previous,), {1 + 2 * N_PIECE: 0}

        def kernel(*refs):
            refs = refs[: 1 + 2 * N_PIECE] + refs[2 + 2 * N_PIECE :]
            correlate_kernel(half, spectra, *refs)

    return pl.pallas_call(
        kernel,
        out_shape=jax.ShapeDtypeStruct((64, 1, 64, 2, 256), jnp.float32),
        grid=(4,),
        in_specs=[smem] + [vmem] * (2 * N_PIECE) + [pl.BlockSpec(memory_space=pl.ANY)] * len(extra),
        out_specs=pl.BlockSpec((16, 1, 64, 2, LANES), lambda i: (i, 0, 0, 0, half)),
        scratch_shapes=[
            pltpu.VMEM((LANES * ROWS, LANES), jnp.float32),
            pltpu.VMEM((LANES, LANES), jnp.float32),
        ],
        input_output_aliases=aliases,
        compiler_params=pltpu.CompilerParams(vmem_limit_bytes=VMEM_LIMIT),
        cost_estimate=pl.CostEstimate(
            flops=2 * 64 * 128 * 256 * 128, bytes_accessed=12 << 20, transcendentals=0
        ),
        name="correlate",
    )(place, *early, *late, *extra)


def ring(value, axis, step):
    count = lax.axis_size(axis)
    return lax.ppermute(value, axis, [(i, (i + step) % count) for i in range(count)])


def spread(own, own8):
    x_size = 4
    below = ring(own, "y", 1)
    above = ring(own, "y", -1)
    sib8 = ring(own8, "core", 1)
    pair = jnp.stack([own8, sib8])
    swing = []
    for x in range(x_size):
        swing.append((2 * x, 2 * ((x + 1) % x_size)))
        swing.append((2 * x + 1, 2 * ((x - 1) % x_size) + 1))
    got = lax.ppermute(pair, ("x", "core"), swing)
    core = lax.axis_index("core")
    part = lax.dynamic_slice_in_dim(got, core * 64, 64, 1)
    got2 = lax.ppermute(part, ("x", "core"), swing)
    far0 = ring(below[:64], "y", 1)
    far1 = ring(above[64:], "y", -1)
    swap = ring(got, "core", 1)
    swap2 = ring(got2, "core", 1)
    return own, below, above, far0, far1, own8, sib8, got, got2, swap, swap2


def shards(frames, tail_frames, prototype):
    spectra = 128
    coeff = jnp.repeat(prototype.reshape(TAPS, CHAN // LANES, LANES), 2, axis=1)
    table = dft_table()

    def words(value):
        shape = value.shape[:2]
        value = value.reshape(shape + (2, CHAN // LANES, LANES)).transpose(0, 1, 3, 2, 4)
        return value.reshape(shape + (16, LANES))

    mine, tail = words(frames), words(tail_frames)
    bands = lax.axis_size("zl")
    following = lax.ppermute(mine[:, : TAPS - 1], "zl", [(b + 1, b) for b in range(bands - 1)])
    is_last = (lax.axis_index("zl") == bands - 1).astype(jnp.int32).reshape(1)
    group = lax.axis_index("zh").reshape(1)
    my_x, my_core = lax.axis_index("x"), lax.axis_index("core")
    toward = 1 - 2 * my_core
    near = lax.rem(my_x - toward + 4, 4)
    other = lax.rem(my_x + toward + 4, 4)
    far = lax.rem(my_x + 2, 4)
    rest = 1 - my_core
    order = [
        2 * my_x + my_core,
        2 * my_x + rest,
        2 * near + my_core,
        2 * near + rest,
        2 * other + rest,
        2 * other + my_core,
    ]
    place = jnp.stack([lax.axis_index("y"), *order, 2 * far, 2 * far + 1, my_core]).astype(jnp.int32)

    early = filter_transform(False, coeff, table, mine)
    late = filter_transform(True, coeff, table, mine, following, tail, is_last)
    out = None
    for half in range(2):
        pieces = []
        for source in (early, late):
            recv = lax.all_to_all(source[half], ("zh", "zl"), 0, 0, tiled=True)
            own, own8 = turn(group, recv)
            pieces.append(spread(own, own8))
        out = correlate(half, spectra, place, *pieces, out)
    return out


def solution(mesh):
    fine = Mesh(mesh.devices.reshape(4, 2, 4, 2, 4), ("x", "core", "y", "zh", "zl"))
    row_col = ("x", "core", "y", "zh")
    placed = (P(row_col, "zl", None, None), P(row_col, None, None, None), P())
    return jax.shard_map(
        shards,
        mesh=fine,
        in_specs=placed,
        out_specs=P(("x", "core"), ("y", "zh"), None, None, "zl"),
        check_vma=False,
    )
```

```python
import functools
import math

import jax
import jax.numpy as jnp
import numpy as np
from jax import lax
from jax.experimental import pallas as pl
from jax.experimental.pallas import tpu as pltpu
from jax.sharding import Mesh
from jax.sharding import PartitionSpec as P

LANES = 128
TAPS = 16
HALF = 16
INPUTS = 8
BANDS = 4
CHAN = 1024
VMEM_LIMIT = 60 * 1024 * 1024
PAIRS = 64


def dft_table():
    sample = np.arange(CHAN, dtype=np.int64)[:, None]
    channel = np.arange(CHAN, dtype=np.int64)[None, :]
    theta = np.float32(2.0 * math.pi / CHAN) * (sample * channel % CHAN).astype(np.float32)
    parts = []
    for trig in (np.cos, np.sin):
        full = trig(theta.astype(np.float64)).astype(np.float32)
        parts.append(full.reshape(CHAN, BANDS, CHAN // BANDS))
    table = np.stack(parts, 2).transpose(1, 0, 2, 3)
    return jnp.asarray(table.reshape(BANDS, CHAN, 2 * CHAN // BANDS), dtype=jnp.bfloat16)


def filter_transform_kernel(late, *refs):
    place_ref, refs = refs[0], refs[1:]
    n_frames = 3 if late else 1
    sources, (proto_ref, table_ref), refs = refs[:n_frames], refs[n_frames : n_frames + 2], refs[n_frames + 2 :]
    held, (table, coeff, sums, lhs, sems, table_sem) = refs[-6 - n_frames : -6], refs[-6:]
    outs = refs[: -6 - n_frames]
    band = place_ref[0]

    def copies(a):
        found = []
        for i, (source, buffer) in enumerate(zip(sources, held)):
            part = source.at[a, HALF:] if late and i == 0 else source.at[a]
            found.append(pltpu.make_async_copy(part, buffer.at[a], sems.at[i, a]))
        return found

    for a in range(INPUTS):
        for copy in copies(a):
            copy.start()

    def table_copy(k):
        return pltpu.make_async_copy(table_ref.at[k], table.at[k], table_sem.at[k])

    for k in range(BANDS):
        table_copy(k).start()
    for k in range(CHAN // LANES):
        for c in range(2):
            coeff[pl.ds(2 * k + c, TAPS, 16), :] = proto_ref[:, k * LANES : (k + 1) * LANES]

    def frame(a, t):
        if t < HALF or not late:
            return held[0][a, t].astype(jnp.float32)
        t -= HALF
        return jnp.where(band == BANDS - 1, held[2][a, t], held[1][a, t]).astype(jnp.float32)

    def one_input(a, carry):
        for copy in copies(a):
            copy.wait()
        acc = [None] * HALF
        for t in range(HALF + TAPS - 1):
            value = frame(a, t)
            for s in range(max(0, t - TAPS + 1), min(HALF, t + 1)):
                term = coeff[(t - s) * 16 : (t - s + 1) * 16, :] * value
                acc[s] = term if acc[s] is None else acc[s] + term
        for s in range(HALF):
            sums[pl.ds(s * 16, 16), :] = acc[s]
        for k in range(CHAN // LANES):
            for c in range(2):
                rows = sums[pl.ds(2 * k + c, HALF, 16), :]
                start = pl.multiple_of((a * 2 + c) * HALF, HALF)
                lhs[pl.ds(start, HALF), k * LANES : (k + 1) * LANES] = rows.astype(jnp.bfloat16)
        return carry

    lax.fori_loop(0, INPUTS, one_input, 0)
    scale = 1.0 / math.sqrt(CHAN)
    width = CHAN // BANDS
    for k in range(BANDS):
        table_copy(k).wait()
        both = jnp.dot(lhs[...], table[k], preferred_element_type=jnp.float32)
        both = both.reshape(INPUTS, 2, HALF, 2 * width)
        real = (both[:, 0, :, :width] + both[:, 1, :, width:]) * scale
        imag = (both[:, 1, :, :width] - both[:, 0, :, width:]) * scale
        for part, value in enumerate((real, imag)):
            value = value.astype(jnp.bfloat16)
            for z in range(2):
                outs[0][z * BANDS + k, :, part] = value


def filter_transform(late, place, prototype, table, *frames):
    vmem = pl.BlockSpec(memory_space=pltpu.VMEM)
    hbm = pl.BlockSpec(memory_space=pl.ANY)
    shapes = [(2 * BANDS, INPUTS, 2, HALF, 2 * LANES)]
    held = [(INPUTS, HALF, 16, LANES)] + [(INPUTS, TAPS - 1, 16, LANES)] * 2
    held = held if late else [(INPUTS, 2 * HALF, 16, LANES)]
    (blocks,) = pl.pallas_call(
        functools.partial(filter_transform_kernel, late),
        out_shape=[jax.ShapeDtypeStruct(shape, jnp.bfloat16) for shape in shapes],
        in_specs=[pl.BlockSpec(memory_space=pltpu.SMEM)] + [hbm] * len(frames) + [vmem, hbm],
        out_specs=[vmem] * len(shapes),
        scratch_shapes=[pltpu.VMEM(shape, jnp.bfloat16) for shape in held]
        + [
            pltpu.VMEM((BANDS, CHAN, 4 * LANES), jnp.bfloat16),
            pltpu.VMEM((TAPS * 16, LANES), jnp.float32),
            pltpu.VMEM((HALF * 16, LANES), jnp.float32),
            pltpu.VMEM((INPUTS * 2 * HALF, CHAN), jnp.bfloat16),
            pltpu.SemaphoreType.DMA((len(held), INPUTS)),
            pltpu.SemaphoreType.DMA((BANDS,)),
        ],
        compiler_params=pltpu.CompilerParams(vmem_limit_bytes=VMEM_LIMIT),
        cost_estimate=pl.CostEstimate(
            flops=FAR if late else 1 << 31, bytes_accessed=8 << 20, transcendentals=0
        ),
        name="filter_transform",
    )(place, *frames, prototype, table)
    return blocks


def turn_kernel(place_ref, recv_ref, *refs):
    outs, own_ref, rows = refs[-4:-2], refs[-2], refs[-1]
    for z in range(2):
        for a in range(INPUTS):
            for g in range(2):
                cols = slice(g * LANES, (g + 1) * LANES)
                pieces = [recv_ref[z * BANDS + k, a, c, :, cols] for c in range(2) for k in range(BANDS)]
                block = jnp.concatenate(pieces, 0).astype(jnp.float32).T
                for h in range(2):
                    start = (g * 2 + z) * PAIRS * 16 + h * INPUTS + a
                    rows[pl.ds(start, PAIRS, 16), :] = block[h * PAIRS : (h + 1) * PAIRS]
    for g in range(2):
        for z in range(2):

            def one(n, carry):
                base = pl.multiple_of(((g * 2 + z) * PAIRS + n) * 16, 16)
                outs[g][z, n] = rows[pl.ds(base, 16), :].astype(jnp.bfloat16)
                return carry

            lax.fori_loop(0, PAIRS, one, 0, unroll=16)
        own_ref[g] = outs[g][place_ref[2]]


def turn(place, recv, *tokens):
    vmem = pl.BlockSpec(memory_space=pltpu.VMEM)
    shapes = [(2, PAIRS, 16, LANES)] * 3
    return pl.pallas_call(
        turn_kernel,
        out_shape=[jax.ShapeDtypeStruct(shape, jnp.bfloat16) for shape in shapes],
        in_specs=[pl.BlockSpec(memory_space=pltpu.SMEM), vmem]
        + [pl.BlockSpec(memory_space=pl.ANY)] * len(tokens),
        out_specs=[vmem] * len(shapes),
        scratch_shapes=[pltpu.VMEM((4 * PAIRS * 16, LANES), jnp.float32)],
        compiler_params=pltpu.CompilerParams(vmem_limit_bytes=32 << 20),
        cost_estimate=pl.CostEstimate(flops=1 << 20, bytes_accessed=4 << 20, transcendentals=0),
        name="turn",
    )(place, recv, *tokens)


STEPS = 2
FAR = 1 << 37


def correlate_kernel(spectra, shape, place_ref, *refs):
    sources, (out_ref, outer, mixed) = refs[: len(shape)], refs[-3:]
    step = pl.program_id(0)
    count = PAIRS // STEPS
    lane = lax.broadcasted_iota(jnp.int32, (1, LANES), 1)
    sign = jnp.where(lane < LANES // 2, -1.0, 1.0)
    first = (lane % 16) < 8

    def multiply(n, carry):
        found = {}
        for ref, (kind, late, blocks) in zip(sources, shape):
            for i in range(blocks):
                at = place_ref[3 + i] if blocks == 8 else i
                value = ref[at, 0, n] if len(ref.shape) == 5 else ref[at, n]
                found.setdefault((kind, late), []).append(value)
        lhs, plain = (
            [jnp.concatenate(found[kind, late], 0) for late in range(2)] for kind in range(2)
        )
        lhs = jnp.concatenate(lhs, 1)
        turned = [
            (pltpu.roll(p.astype(jnp.float32), LANES // 2, 1) * sign).astype(jnp.bfloat16)
            for p in plain
        ]
        rhs = jnp.concatenate([jnp.concatenate(plain, 1), jnp.concatenate(turned, 1)], 0)
        value = lax.dot_general(
            lhs, rhs, (((1,), (1,)), ((), ())), preferred_element_type=jnp.float32
        )
        value = value.reshape(8, 2, 8, 2 * LANES)
        base = (step * count + n) * 64
        for part in range(2):
            cols = slice(part * LANES, (part + 1) * LANES)
            kept = jnp.where(first[None], value[:, 0, :, cols], value[:, 1, :, cols])
            outer[part, pl.ds(pl.multiple_of(base, 64), 64), :] = kept.reshape(64, LANES)
        return carry

    @pl.when(step < STEPS)
    def _():
        lax.fori_loop(0, count, multiply, 0, unroll=16)

    low = lane < LANES // 2

    def write(i, carry):
        place = lax.rem(step - STEPS - place_ref[1] + 4, 4) * 16
        for part in range(2):
            cols = [outer[part, pl.ds(place + z * 8 + i, PAIRS, 64), :] for z in range(2)]
            block = jnp.concatenate(cols, 0).T * (1.0 / spectra)
            for r in range(8):
                start = place_ref[3 + r] * 16 + part
                one = block[r * 16 : r * 16 + 8]
                two = block[r * 16 + 8 : r * 16 + 16]
                near = jnp.where(low, one, pltpu.roll(two, PAIRS, 1))
                other = jnp.where(low, pltpu.roll(one, PAIRS, 1), two)
                mixed[0, pl.ds(start, 8, 2), :] = near
                mixed[1, pl.ds(start, 8, 2), :] = other
        for z in range(2):
            out_ref[i + z * 8, 0] = mixed[z].reshape(64, 2, LANES)
        return carry

    @pl.when(step >= STEPS)
    def _():
        lax.fori_loop(0, 8, write, 0, unroll=4)


def correlate(half, spectra, place, lefts, rights, previous):
    count = PAIRS // STEPS
    arrays, shape = [], []
    for kind, both in enumerate((lefts, rights)):
        for late, values in enumerate(both):
            for value in values:
                arrays.append(value)
                shape.append((kind, late, value.shape[0]))
    specs = []
    for value in arrays:
        lead = value.shape[:-3]
        at = (0, half if lead[-1] == 2 else 0) if len(lead) == 2 else (0,)
        size = (lead[0],) + (1,) * (len(lead) - 1)

        def index(i, at=at):
            return (*at, jnp.minimum(i, STEPS - 1), 0, 0)

        specs.append(pl.BlockSpec((*size, count, 16, LANES), index))
    n_in = 1 + len(arrays)
    extra, aliases = (), {}
    kernel = functools.partial(correlate_kernel, spectra, shape)
    if previous is not None:
        extra, aliases = (previous,), {n_in: 0}

        def kernel(*refs):
            correlate_kernel(spectra, shape, *refs[:n_in], *refs[n_in + 1 :])

    return pl.pallas_call(
        kernel,
        out_shape=jax.ShapeDtypeStruct((64, 1, 64, 2, 256), jnp.float32),
        grid=(STEPS + 4,),
        in_specs=[pl.BlockSpec(memory_space=pltpu.SMEM)]
        + specs
        + [pl.BlockSpec(memory_space=pl.ANY)] * len(extra),
        out_specs=pl.BlockSpec(
            (16, 1, 64, 2, LANES), lambda i: (jnp.maximum(i - STEPS, 0), 0, 0, 0, half)
        ),
        scratch_shapes=[
            pltpu.VMEM((2, PAIRS * 64, LANES), jnp.float32),
            pltpu.VMEM((2, LANES, LANES), jnp.float32),
        ],
        input_output_aliases=aliases,
        compiler_params=pltpu.CompilerParams(vmem_limit_bytes=VMEM_LIMIT),
        cost_estimate=pl.CostEstimate(
            flops=2 * 64 * 128 * 256 * 128, bytes_accessed=12 << 20, transcendentals=0
        ),
        name="correlate",
    )(place, *arrays, *extra)


def hold_kernel(*refs):
    refs[-1][...] = jnp.zeros_like(refs[-1])


def hold(*values):
    return pl.pallas_call(
        hold_kernel,
        out_shape=jax.ShapeDtypeStruct((8, LANES), jnp.float32),
        in_specs=[pl.BlockSpec(memory_space=pl.ANY)] * len(values),
        out_specs=pl.BlockSpec(memory_space=pltpu.VMEM),
        compiler_params=pltpu.CompilerParams(vmem_limit_bytes=60 << 20),
        cost_estimate=pl.CostEstimate(flops=FAR, bytes_accessed=1 << 20, transcendentals=0),
        name="hold",
    )(*values)


def ring(value, axis, step):
    count = lax.axis_size(axis)
    return lax.ppermute(value, axis, [(i, (i + step) % count) for i in range(count)])


def along_y(value, step):
    below, above = ring(value, "y", 1), ring(value, "y", -1)
    return value, above, ring(below if step > 0 else above, "y", step), below


def across_x(own):
    found = []
    for step in range(4):
        same = ring(own, "x", -step) if step else own
        found += [same, ring(same, "core", 1)]
    return [value[None] for value in found]


def gather_x(own):
    return [lax.all_gather(own, ("x", "core"), axis=0)]


def shards(frames, tail_frames, prototype):
    spectra = 128
    table = dft_table()

    def words(value):
        shape = value.shape[:2]
        value = value.reshape(shape + (2, CHAN // LANES, LANES)).transpose(0, 1, 3, 2, 4)
        return value.reshape(shape + (16, LANES))

    mine, tail = words(frames), words(tail_frames)
    bands = lax.axis_size("zl")
    following = lax.ppermute(mine[:, : TAPS - 1], "zl", [(b + 1, b) for b in range(bands - 1)])
    place = [lax.axis_index(axis) for axis in ("zl", "y", "zh")]
    my_x, my_core = lax.axis_index("x"), lax.axis_index("core")
    order = []
    for step in range(4):
        there = lax.rem(my_x + step, 4) * 2
        order += [there + my_core, there + 1 - my_core]
    place = jnp.stack(place + order).astype(jnp.int32)

    early = filter_transform(False, place, prototype, table, mine)
    late = filter_transform(True, place, prototype, table, mine, following, tail)

    exchange = functools.partial(
        lax.all_to_all, axis_name=("zh", "zl"), split_axis=0, concat_axis=0, tiled=True
    )
    recv, late = lax.optimization_barrier((exchange(early), late))
    *halves, own = turn(place, recv)
    right0 = gather_x(own)
    first = [along_y(value, step) for value, step in zip(halves, (1, -1))]
    near = [value for _, above, _, below in first for value in (above, below)]
    tokens = hold(*near), hold(first[0][2], first[1][2])
    *halves, own = turn(place, exchange(late), *tokens)
    right1 = across_x(own)
    second = [along_y(value, step) for value, step in zip(halves, (1, -1))]
    out = None
    for half in range(2):
        out = correlate(half, spectra, place, (first[half], second[half]), (right0, right1), out)
    return out


def solution(mesh):
    fine = Mesh(mesh.devices.reshape(4, 2, 4, 2, 4), ("x", "core", "y", "zh", "zl"))
    row_col = ("x", "core", "y", "zh")
    placed = (P(row_col, "zl", None, None), P(row_col, None, None, None), P())
    return jax.shard_map(
        shards,
        mesh=fine,
        in_specs=placed,
        out_specs=P(("x", "core"), ("y", "zh"), None, None, "zl"),
        check_vma=False,
    )
```

```python
import functools
import math

import jax
import jax.numpy as jnp
import numpy as np
from jax import lax
from jax.experimental import pallas as pl
from jax.experimental.pallas import tpu as pltpu
from jax.sharding import Mesh
from jax.sharding import PartitionSpec as P

LANES = 128
TAPS = 16
HALF = 16
INPUTS = 8
BANDS = 4
CHAN = 1024
VMEM_LIMIT = 60 * 1024 * 1024
PAIRS = 64


def dft_table():
    sample = np.arange(CHAN, dtype=np.int64)[:, None]
    channel = np.arange(CHAN, dtype=np.int64)[None, :]
    theta = np.float32(2.0 * math.pi / CHAN) * (sample * channel % CHAN).astype(np.float32)
    parts = []
    for trig in (np.cos, np.sin):
        full = trig(theta.astype(np.float64)).astype(np.float32)
        parts.append(full.reshape(CHAN, BANDS, CHAN // BANDS))
    table = np.stack(parts, 2).transpose(1, 0, 2, 3)
    return jnp.asarray(table.reshape(BANDS, CHAN, 2 * CHAN // BANDS), dtype=jnp.bfloat16)


def filter_transform_kernel(late, *refs):
    place_ref, refs = refs[0], refs[1:]
    n_frames = 3 if late else 1
    sources, (proto_ref, table_ref), refs = refs[:n_frames], refs[n_frames : n_frames + 2], refs[n_frames + 2 :]
    held, (table, coeff, sums, lhs, sems, table_sem) = refs[-6 - n_frames : -6], refs[-6:]
    outs = refs[: -6 - n_frames]
    band = place_ref[0]

    def copies(a):
        found = []
        for i, (source, buffer) in enumerate(zip(sources, held)):
            part = source.at[a, HALF:] if late and i == 0 else source.at[a]
            found.append(pltpu.make_async_copy(part, buffer.at[a], sems.at[i, a]))
        return found

    for a in range(INPUTS):
        for copy in copies(a):
            copy.start()

    def table_copy(k):
        return pltpu.make_async_copy(table_ref.at[k], table.at[k], table_sem.at[k])

    for k in range(BANDS):
        table_copy(k).start()
    for k in range(CHAN // LANES):
        for c in range(2):
            coeff[pl.ds(2 * k + c, TAPS, 16), :] = proto_ref[:, k * LANES : (k + 1) * LANES]

    def frame(a, t):
        if t < HALF or not late:
            return held[0][a, t].astype(jnp.float32)
        t -= HALF
        return jnp.where(band == BANDS - 1, held[2][a, t], held[1][a, t]).astype(jnp.float32)

    def one_input(a, carry):
        for copy in copies(a):
            copy.wait()
        acc = [None] * HALF
        for t in range(HALF + TAPS - 1):
            value = frame(a, t)
            for s in range(max(0, t - TAPS + 1), min(HALF, t + 1)):
                term = coeff[(t - s) * 16 : (t - s + 1) * 16, :] * value
                acc[s] = term if acc[s] is None else acc[s] + term
        for s in range(HALF):
            sums[pl.ds(s * 16, 16), :] = acc[s]
        for k in range(CHAN // LANES):
            for c in range(2):
                rows = sums[pl.ds(2 * k + c, HALF, 16), :]
                start = pl.multiple_of((a * 2 + c) * HALF, HALF)
                lhs[pl.ds(start, HALF), k * LANES : (k + 1) * LANES] = rows.astype(jnp.bfloat16)
        return carry

    lax.fori_loop(0, INPUTS, one_input, 0)
    scale = 1.0 / math.sqrt(CHAN)
    width = CHAN // BANDS
    for k in range(BANDS):
        table_copy(k).wait()
        both = jnp.dot(lhs[...], table[k], preferred_element_type=jnp.float32)
        both = both.reshape(INPUTS, 2, HALF, 2 * width)
        real = (both[:, 0, :, :width] + both[:, 1, :, width:]) * scale
        imag = (both[:, 1, :, :width] - both[:, 0, :, width:]) * scale
        for part, value in enumerate((real, imag)):
            value = value.astype(jnp.bfloat16)
            for half, out in enumerate(outs):
                cols = slice(half * LANES, (half + 1) * LANES) if late else slice(None)
                for z in range(2):
                    out[z * BANDS + k, :, part] = value[:, :, cols]


def filter_transform(late, place, prototype, table, *frames):
    vmem = pl.BlockSpec(memory_space=pltpu.VMEM)
    hbm = pl.BlockSpec(memory_space=pl.ANY)
    shapes = [(2 * BANDS, INPUTS, 2, HALF, LANES if late else 2 * LANES)] * (1 + late)
    held = [(INPUTS, HALF, 16, LANES)] + [(INPUTS, TAPS - 1, 16, LANES)] * 2
    held = held if late else [(INPUTS, 2 * HALF, 16, LANES)]
    return pl.pallas_call(
        functools.partial(filter_transform_kernel, late),
        out_shape=[jax.ShapeDtypeStruct(shape, jnp.bfloat16) for shape in shapes],
        in_specs=[pl.BlockSpec(memory_space=pltpu.SMEM)] + [hbm] * len(frames) + [vmem, hbm],
        out_specs=[vmem] * len(shapes),
        scratch_shapes=[pltpu.VMEM(shape, jnp.bfloat16) for shape in held]
        + [
            pltpu.VMEM((BANDS, CHAN, 4 * LANES), jnp.bfloat16),
            pltpu.VMEM((TAPS * 16, LANES), jnp.float32),
            pltpu.VMEM((HALF * 16, LANES), jnp.float32),
            pltpu.VMEM((INPUTS * 2 * HALF, CHAN), jnp.bfloat16),
            pltpu.SemaphoreType.DMA((len(held), INPUTS)),
            pltpu.SemaphoreType.DMA((BANDS,)),
        ],
        compiler_params=pltpu.CompilerParams(vmem_limit_bytes=VMEM_LIMIT),
        cost_estimate=pl.CostEstimate(
            flops=FAR if late else 1 << 31, bytes_accessed=8 << 20, transcendentals=0
        ),
        name="filter_transform",
    )(place, *frames, prototype, table)


def turn_kernel(place_ref, recv_ref, *refs):
    halves = recv_ref.shape[-1] // LANES
    outs, own_ref, rows = refs[-2 - halves : -2], refs[-2], refs[-1]
    for z in range(2):
        for a in range(INPUTS):
            for g in range(halves):
                cols = slice(g * LANES, (g + 1) * LANES)
                pieces = [recv_ref[z * BANDS + k, a, c, :, cols] for c in range(2) for k in range(BANDS)]
                block = jnp.concatenate(pieces, 0).astype(jnp.float32).T
                for h in range(2):
                    start = (g * 2 + z) * PAIRS * 16 + h * INPUTS + a
                    rows[pl.ds(start, PAIRS, 16), :] = block[h * PAIRS : (h + 1) * PAIRS]
    for g in range(halves):
        for z in range(2):

            def one(n, carry):
                base = pl.multiple_of(((g * 2 + z) * PAIRS + n) * 16, 16)
                outs[g][z, n] = rows[pl.ds(base, 16), :].astype(jnp.bfloat16)
                return carry

            lax.fori_loop(0, PAIRS, one, 0, unroll=16)
        own_ref[g] = outs[g][place_ref[2]]


def turn(place, recv, *tokens):
    vmem = pl.BlockSpec(memory_space=pltpu.VMEM)
    halves = recv.shape[-1] // LANES
    shapes = [(2, PAIRS, 16, LANES)] * halves + [(halves, PAIRS, 16, LANES)]
    return pl.pallas_call(
        turn_kernel,
        out_shape=[jax.ShapeDtypeStruct(shape, jnp.bfloat16) for shape in shapes],
        in_specs=[pl.BlockSpec(memory_space=pltpu.SMEM), vmem]
        + [pl.BlockSpec(memory_space=pl.ANY)] * len(tokens),
        out_specs=[vmem] * len(shapes),
        scratch_shapes=[pltpu.VMEM((2 * halves * PAIRS * 16, LANES), jnp.float32)],
        compiler_params=pltpu.CompilerParams(vmem_limit_bytes=32 << 20),
        cost_estimate=pl.CostEstimate(flops=1 << 20, bytes_accessed=4 << 20, transcendentals=0),
        name="turn",
    )(place, recv, *tokens)


STEPS = 2
FAR = 1 << 37


def correlate_kernel(spectra, shape, place_ref, *refs):
    sources, (out_ref, outer, mixed) = refs[: len(shape)], refs[-3:]
    step = pl.program_id(0)
    count = PAIRS // STEPS
    lane = lax.broadcasted_iota(jnp.int32, (1, LANES), 1)
    sign = jnp.where(lane < LANES // 2, -1.0, 1.0)
    first = (lane % 16) < 8

    def multiply(n, carry):
        found = {}
        for ref, (kind, late, blocks) in zip(sources, shape):
            for i in range(blocks):
                at = place_ref[3 + i] if blocks == 8 else i
                value = ref[at, 0, n] if len(ref.shape) == 5 else ref[at, n]
                found.setdefault((kind, late), []).append(value)
        lhs, plain = (
            [jnp.concatenate(found[kind, late], 0) for late in range(2)] for kind in range(2)
        )
        lhs = jnp.concatenate(lhs, 1)
        turned = [
            (pltpu.roll(p.astype(jnp.float32), LANES // 2, 1) * sign).astype(jnp.bfloat16)
            for p in plain
        ]
        rhs = jnp.concatenate([jnp.concatenate(plain, 1), jnp.concatenate(turned, 1)], 0)
        value = lax.dot_general(
            lhs, rhs, (((1,), (1,)), ((), ())), preferred_element_type=jnp.float32
        )
        value = value.reshape(8, 2, 8, 2 * LANES)
        base = (step * count + n) * 64
        for part in range(2):
            cols = slice(part * LANES, (part + 1) * LANES)
            kept = jnp.where(first[None], value[:, 0, :, cols], value[:, 1, :, cols])
            outer[part, pl.ds(pl.multiple_of(base, 64), 64), :] = kept.reshape(64, LANES)
        return carry

    @pl.when(step < STEPS)
    def _():
        lax.fori_loop(0, count, multiply, 0, unroll=16)

    low = lane < LANES // 2

    def write(i, carry):
        place = lax.rem(step - STEPS - place_ref[1] + 4, 4) * 16
        for part in range(2):
            cols = [outer[part, pl.ds(place + z * 8 + i, PAIRS, 64), :] for z in range(2)]
            block = jnp.concatenate(cols, 0).T * (1.0 / spectra)
            for r in range(8):
                start = place_ref[3 + r] * 16 + part
                one = block[r * 16 : r * 16 + 8]
                two = block[r * 16 + 8 : r * 16 + 16]
                near = jnp.where(low, one, pltpu.roll(two, PAIRS, 1))
                other = jnp.where(low, pltpu.roll(one, PAIRS, 1), two)
                mixed[0, pl.ds(start, 8, 2), :] = near
                mixed[1, pl.ds(start, 8, 2), :] = other
        for z in range(2):
            out_ref[i + z * 8, 0] = mixed[z].reshape(64, 2, LANES)
        return carry

    @pl.when(step >= STEPS)
    def _():
        lax.fori_loop(0, 8, write, 0, unroll=4)


def correlate(half, spectra, place, lefts, rights, previous):
    count = PAIRS // STEPS
    arrays, shape = [], []
    for kind, both in enumerate((lefts, rights)):
        for late, values in enumerate(both):
            for value in values:
                arrays.append(value)
                shape.append((kind, late, value.shape[0]))
    specs = []
    for value in arrays:
        lead = value.shape[:-3]
        at = (0, half if lead[-1] == 2 else 0) if len(lead) == 2 else (0,)
        size = (lead[0],) + (1,) * (len(lead) - 1)

        def index(i, at=at):
            return (*at, jnp.minimum(i, STEPS - 1), 0, 0)

        specs.append(pl.BlockSpec((*size, count, 16, LANES), index))
    n_in = 1 + len(arrays)
    extra, aliases = (), {}
    kernel = functools.partial(correlate_kernel, spectra, shape)
    if previous is not None:
        extra, aliases = (previous,), {n_in: 0}

        def kernel(*refs):
            correlate_kernel(spectra, shape, *refs[:n_in], *refs[n_in + 1 :])

    return pl.pallas_call(
        kernel,
        out_shape=jax.ShapeDtypeStruct((64, 1, 64, 2, 256), jnp.float32),
        grid=(STEPS + 4,),
        in_specs=[pl.BlockSpec(memory_space=pltpu.SMEM)]
        + specs
        + [pl.BlockSpec(memory_space=pl.ANY)] * len(extra),
        out_specs=pl.BlockSpec(
            (16, 1, 64, 2, LANES), lambda i: (jnp.maximum(i - STEPS, 0), 0, 0, 0, half)
        ),
        scratch_shapes=[
            pltpu.VMEM((2, PAIRS * 64, LANES), jnp.float32),
            pltpu.VMEM((2, LANES, LANES), jnp.float32),
        ],
        input_output_aliases=aliases,
        compiler_params=pltpu.CompilerParams(vmem_limit_bytes=VMEM_LIMIT),
        cost_estimate=pl.CostEstimate(
            flops=1 << 33, bytes_accessed=12 << 20, transcendentals=0
        ),
        name="correlate",
    )(place, *arrays, *extra)


def ring(value, axis, step):
    count = lax.axis_size(axis)
    return lax.ppermute(value, axis, [(i, (i + step) % count) for i in range(count)])


def along_y(value, step):
    below, above = ring(value, "y", 1), ring(value, "y", -1)
    return value, above, ring(below if step > 0 else above, "y", step), below


def across_x(own):
    found = []
    for step in range(4):
        same = ring(own, "x", -step) if step else own
        found += [same, ring(same, "core", 1)]
    return [value[None] for value in found]


def gather_x(own):
    return [lax.all_gather(own, ("x", "core"), axis=0)]


def shards(frames, tail_frames, prototype):
    spectra = 128
    table = dft_table()

    def words(value):
        shape = value.shape[:2]
        value = value.reshape(shape + (2, CHAN // LANES, LANES)).transpose(0, 1, 3, 2, 4)
        return value.reshape(shape + (16, LANES))

    mine, tail = words(frames), words(tail_frames)
    bands = lax.axis_size("zl")
    following = lax.ppermute(mine[:, : TAPS - 1], "zl", [(b + 1, b) for b in range(bands - 1)])
    place = [lax.axis_index(axis) for axis in ("zl", "y", "zh")]
    my_x, my_core = lax.axis_index("x"), lax.axis_index("core")
    order = []
    for step in range(4):
        there = lax.rem(my_x + step, 4) * 2
        order += [there + my_core, there + 1 - my_core]
    place = jnp.stack(place + order).astype(jnp.int32)

    early = filter_transform(False, place, prototype, table, mine)
    late = filter_transform(True, place, prototype, table, mine, following, tail)

    exchange = functools.partial(
        lax.all_to_all, axis_name=("zh", "zl"), split_axis=0, concat_axis=0, tiled=True
    )
    recv, *late = lax.optimization_barrier((exchange(early[0]), *late))
    *halves, own = turn(place, recv)
    right0 = gather_x(own)
    first = [along_y(value, step) for value, step in zip(halves, (1, -1))]
    recv, last = lax.optimization_barrier((exchange(late[0]), late[1]))

    value, own = turn(place, recv)
    second = [along_y(value, -1)]
    right1 = [across_x(own)]

    value, own = turn(place, exchange(last))
    second.append(along_y(value, 1))
    right1.append(across_x(own))
    out = None
    for half in range(2):
        lefts, rights = (first[half], second[half]), (right0, right1[half])
        out = correlate(half, spectra, place, lefts, rights, out)
    return out


def solution(mesh):
    fine = Mesh(mesh.devices.reshape(4, 2, 4, 2, 4), ("x", "core", "y", "zh", "zl"))
    row_col = ("x", "core", "y", "zh")
    placed = (P(row_col, "zl", None, None), P(row_col, None, None, None), P())
    return jax.shard_map(
        shards,
        mesh=fine,
        in_specs=placed,
        out_specs=P(("x", "core"), ("y", "zh"), None, None, "zl"),
        check_vma=False,
    )
```

```python
import functools
import math

import jax
import jax.numpy as jnp
import numpy as np
from jax import lax
from jax.experimental import pallas as pl
from jax.experimental.pallas import tpu as pltpu
from jax.sharding import Mesh
from jax.sharding import PartitionSpec as P

LANES = 128
TAPS = 16
HALF = 16
INPUTS = 8
BANDS = 4
CHAN = 1024
VMEM_LIMIT = 60 * 1024 * 1024
PAIRS = 64


def dft_table():
    sample = np.arange(CHAN, dtype=np.int64)[:, None]
    channel = np.arange(CHAN, dtype=np.int64)[None, :]
    theta = np.float32(2.0 * math.pi / CHAN) * (sample * channel % CHAN).astype(np.float32)
    parts = []
    for trig in (np.cos, np.sin):
        full = trig(theta.astype(np.float64)).astype(np.float32)
        parts.append(full.reshape(CHAN, BANDS, CHAN // BANDS))
    table = np.stack(parts, 2).transpose(1, 0, 2, 3)
    return jnp.asarray(table.reshape(BANDS, CHAN, 2 * CHAN // BANDS), dtype=jnp.bfloat16)


def filter_transform_kernel(late, *refs):
    place_ref, refs = refs[0], refs[1:]
    n_frames = 3 if late else 1
    sources, (proto_ref, table_ref), refs = refs[:n_frames], refs[n_frames : n_frames + 2], refs[n_frames + 2 :]
    held, (table, coeff, sums, lhs, sems, table_sem) = refs[-6 - n_frames : -6], refs[-6:]
    outs = refs[: -6 - n_frames]
    band = place_ref[0]

    def copies(a):
        found = []
        for i, (source, buffer) in enumerate(zip(sources, held)):
            part = source.at[a, HALF:] if late and i == 0 else source.at[a]
            found.append(pltpu.make_async_copy(part, buffer.at[a], sems.at[i, a]))
        return found

    for a in range(INPUTS):
        for copy in copies(a):
            copy.start()

    def table_copy(k):
        return pltpu.make_async_copy(table_ref.at[k], table.at[k], table_sem.at[k])

    for k in range(BANDS):
        table_copy(k).start()
    for k in range(CHAN // LANES):
        for c in range(2):
            coeff[pl.ds(2 * k + c, TAPS, 16), :] = proto_ref[:, k * LANES : (k + 1) * LANES]

    def frame(a, t):
        if t < HALF or not late:
            return held[0][a, t].astype(jnp.float32)
        t -= HALF
        return jnp.where(band == BANDS - 1, held[2][a, t], held[1][a, t]).astype(jnp.float32)

    def one_input(a, carry):
        for copy in copies(a):
            copy.wait()
        acc = [None] * HALF
        for t in range(HALF + TAPS - 1):
            value = frame(a, t)
            for s in range(max(0, t - TAPS + 1), min(HALF, t + 1)):
                term = coeff[(t - s) * 16 : (t - s + 1) * 16, :] * value
                acc[s] = term if acc[s] is None else acc[s] + term
        for s in range(HALF):
            sums[pl.ds(s * 16, 16), :] = acc[s]
        for k in range(CHAN // LANES):
            for c in range(2):
                rows = sums[pl.ds(2 * k + c, HALF, 16), :]
                start = pl.multiple_of((a * 2 + c) * HALF, HALF)
                lhs[pl.ds(start, HALF), k * LANES : (k + 1) * LANES] = rows.astype(jnp.bfloat16)
        return carry

    lax.fori_loop(0, INPUTS, one_input, 0)
    scale = 1.0 / math.sqrt(CHAN)
    width = CHAN // BANDS
    for k in range(BANDS):
        table_copy(k).wait()
        both = jnp.dot(lhs[...], table[k], preferred_element_type=jnp.float32)
        both = both.reshape(INPUTS, 2, HALF, 2 * width)
        real = (both[:, 0, :, :width] + both[:, 1, :, width:]) * scale
        imag = (both[:, 1, :, :width] - both[:, 0, :, width:]) * scale
        for part, value in enumerate((real, imag)):
            value = value.astype(jnp.bfloat16)
            for half, out in enumerate(outs):
                cols = slice(half * LANES, (half + 1) * LANES) if late else slice(None)
                for z in range(2):
                    out[z * BANDS + k, :, part] = value[:, :, cols]


def filter_transform(late, place, prototype, table, *frames):
    vmem = pl.BlockSpec(memory_space=pltpu.VMEM)
    hbm = pl.BlockSpec(memory_space=pl.ANY)
    shapes = [(2 * BANDS, INPUTS, 2, HALF, LANES if late else 2 * LANES)] * (1 + late)
    held = [(INPUTS, HALF, 16, LANES)] + [(INPUTS, TAPS - 1, 16, LANES)] * 2
    held = held if late else [(INPUTS, 2 * HALF, 16, LANES)]
    return pl.pallas_call(
        functools.partial(filter_transform_kernel, late),
        out_shape=[jax.ShapeDtypeStruct(shape, jnp.bfloat16) for shape in shapes],
        in_specs=[pl.BlockSpec(memory_space=pltpu.SMEM)] + [hbm] * len(frames) + [vmem, hbm],
        out_specs=[vmem] * len(shapes),
        scratch_shapes=[pltpu.VMEM(shape, jnp.bfloat16) for shape in held]
        + [
            pltpu.VMEM((BANDS, CHAN, 4 * LANES), jnp.bfloat16),
            pltpu.VMEM((TAPS * 16, LANES), jnp.float32),
            pltpu.VMEM((HALF * 16, LANES), jnp.float32),
            pltpu.VMEM((INPUTS * 2 * HALF, CHAN), jnp.bfloat16),
            pltpu.SemaphoreType.DMA((len(held), INPUTS)),
            pltpu.SemaphoreType.DMA((BANDS,)),
        ],
        compiler_params=pltpu.CompilerParams(vmem_limit_bytes=VMEM_LIMIT),
        cost_estimate=pl.CostEstimate(
            flops=FAR if late else 1 << 31, bytes_accessed=8 << 20, transcendentals=0
        ),
        name="filter_transform",
    )(place, *frames, prototype, table)


def turn_kernel(place_ref, recv_ref, *refs):
    halves = recv_ref.shape[-1] // LANES
    outs, own_ref, rows = refs[-2 - halves : -2], refs[-2], refs[-1]
    for z in range(2):
        for a in range(INPUTS):
            for g in range(halves):
                cols = slice(g * LANES, (g + 1) * LANES)
                pieces = [recv_ref[z * BANDS + k, a, c, :, cols] for c in range(2) for k in range(BANDS)]
                block = jnp.concatenate(pieces, 0).astype(jnp.float32).T
                for h in range(2):
                    start = (g * 2 + z) * PAIRS * 16 + h * INPUTS + a
                    rows[pl.ds(start, PAIRS, 16), :] = block[h * PAIRS : (h + 1) * PAIRS]
    for g in range(halves):
        for z in range(2):

            def one(n, carry):
                base = pl.multiple_of(((g * 2 + z) * PAIRS + n) * 16, 16)
                outs[g][z, n] = rows[pl.ds(base, 16), :].astype(jnp.bfloat16)
                return carry

            lax.fori_loop(0, PAIRS, one, 0, unroll=16)
        own_ref[g] = outs[g][place_ref[2]]


def turn(place, recv, *tokens):
    vmem = pl.BlockSpec(memory_space=pltpu.VMEM)
    halves = recv.shape[-1] // LANES
    shapes = [(2, PAIRS, 16, LANES)] * halves + [(halves, PAIRS, 16, LANES)]
    return pl.pallas_call(
        turn_kernel,
        out_shape=[jax.ShapeDtypeStruct(shape, jnp.bfloat16) for shape in shapes],
        in_specs=[pl.BlockSpec(memory_space=pltpu.SMEM), vmem]
        + [pl.BlockSpec(memory_space=pl.ANY)] * len(tokens),
        out_specs=[vmem] * len(shapes),
        scratch_shapes=[pltpu.VMEM((2 * halves * PAIRS * 16, LANES), jnp.float32)],
        compiler_params=pltpu.CompilerParams(vmem_limit_bytes=32 << 20),
        cost_estimate=pl.CostEstimate(flops=1 << 20, bytes_accessed=4 << 20, transcendentals=0),
        name="turn",
    )(place, recv, *tokens)


STEPS = 2
FAR = 1 << 37


def correlate_kernel(spectra, shape, place_ref, *refs):
    sources, (out_ref, outer, mixed) = refs[: len(shape)], refs[-3:]
    step = pl.program_id(0)
    count = PAIRS // STEPS
    lane = lax.broadcasted_iota(jnp.int32, (1, LANES), 1)
    sign = jnp.where(lane < LANES // 2, 1.0, -1.0)
    first = (lane % 16) < 8

    def multiply(n, carry):
        found = {}
        for ref, (kind, late, blocks) in zip(sources, shape):
            for i in range(blocks):
                at = place_ref[3 + i] if blocks == 8 else i
                value = ref[at, 0, n] if len(ref.shape) == 5 else ref[at, n]
                found.setdefault((kind, late), []).append(value)
        lhs, plain = (
            [jnp.concatenate(found[kind, late], 0) for late in range(2)] for kind in range(2)
        )
        turned = [
            (pltpu.roll(p.astype(jnp.float32), LANES // 2, 1) * sign).astype(jnp.bfloat16)
            for p in lhs
        ]
        lhs = jnp.concatenate([jnp.concatenate(lhs, 1), jnp.concatenate(turned, 1)], 0)
        value = lax.dot_general(
            lhs,
            jnp.concatenate(plain, 1),
            (((1,), (1,)), ((), ())),
            preferred_element_type=jnp.float32,
        )
        value = value.reshape(2, 8, 2, 8, LANES)
        base = (step * count + n) * 64
        for part in range(2):
            kept = jnp.where(first[None], value[part, :, 0], value[part, :, 1])
            outer[part, pl.ds(pl.multiple_of(base, 64), 64), :] = kept.reshape(64, LANES)
        return carry

    @pl.when(step < STEPS)
    def _():
        lax.fori_loop(0, count, multiply, 0, unroll=32)

    low = lane < LANES // 2

    def write(i):
        place = lax.rem(step - STEPS - place_ref[1] + 4, 4) * 16
        for part in range(2):
            cols = [outer[part, pl.ds(place + z * 8 + i, PAIRS, 64), :] for z in range(2)]
            block = jnp.concatenate(cols, 0).T * (1.0 / spectra)
            for r in range(8):
                start = place_ref[3 + r] * 16 + part
                one = block[r * 16 : r * 16 + 8]
                two = block[r * 16 + 8 : r * 16 + 16]
                near = jnp.where(low, one, pltpu.roll(two, PAIRS, 1))
                other = jnp.where(low, pltpu.roll(one, PAIRS, 1), two)
                mixed[i % 2, 0, pl.ds(start, 8, 2), :] = near
                mixed[i % 2, 1, pl.ds(start, 8, 2), :] = other
        for z in range(2):
            out_ref[i + z * 8, 0] = mixed[i % 2, z].reshape(64, 2, LANES)

    @pl.when(step >= STEPS)
    def _():
        for i in range(8):
            write(i)


def correlate(half, spectra, place, lefts, rights, previous):
    count = PAIRS // STEPS
    arrays, shape = [], []
    for kind, both in enumerate((lefts, rights)):
        for late, values in enumerate(both):
            for value in values:
                arrays.append(value)
                shape.append((kind, late, value.shape[0]))
    specs = []
    for value in arrays:
        lead = value.shape[:-3]
        at = (0, half if lead[-1] == 2 else 0) if len(lead) == 2 else (0,)
        size = (lead[0],) + (1,) * (len(lead) - 1)

        def index(i, at=at):
            return (*at, jnp.minimum(i, STEPS - 1), 0, 0)

        specs.append(pl.BlockSpec((*size, count, 16, LANES), index))
    n_in = 1 + len(arrays)
    extra, aliases = (), {}
    kernel = functools.partial(correlate_kernel, spectra, shape)
    if previous is not None:
        extra, aliases = (previous,), {n_in: 0}

        def kernel(*refs):
            correlate_kernel(spectra, shape, *refs[:n_in], *refs[n_in + 1 :])

    return pl.pallas_call(
        kernel,
        out_shape=jax.ShapeDtypeStruct((64, 1, 64, 2, 256), jnp.float32),
        grid=(STEPS + 4,),
        in_specs=[pl.BlockSpec(memory_space=pltpu.SMEM)]
        + specs
        + [pl.BlockSpec(memory_space=pl.ANY)] * len(extra),
        out_specs=pl.BlockSpec(
            (16, 1, 64, 2, LANES), lambda i: (jnp.maximum(i - STEPS, 0), 0, 0, 0, half)
        ),
        scratch_shapes=[
            pltpu.VMEM((2, PAIRS * 64, LANES), jnp.float32),
            pltpu.VMEM((2, 2, LANES, LANES), jnp.float32),
        ],
        input_output_aliases=aliases,
        compiler_params=pltpu.CompilerParams(vmem_limit_bytes=VMEM_LIMIT),
        cost_estimate=pl.CostEstimate(
            flops=1 << 33, bytes_accessed=12 << 20, transcendentals=0
        ),
        name="correlate",
    )(place, *arrays, *extra)


def ring(value, axis, step):
    count = lax.axis_size(axis)
    return lax.ppermute(value, axis, [(i, (i + step) % count) for i in range(count)])


def along_y(value, step):
    below, above = ring(value, "y", 1), ring(value, "y", -1)
    return value, above, ring(below if step > 0 else above, "y", step), below


def across_x(own):
    found = []
    for step in range(4):
        same = ring(own, "x", -step) if step else own
        found += [same, ring(same, "core", 1)]
    return [value[None] for value in found]


def gather_x(own):
    return [lax.all_gather(own, ("x", "core"), axis=0)]


def shards(frames, tail_frames, prototype):
    spectra = 128
    table = dft_table()

    def words(value):
        shape = value.shape[:2]
        value = value.reshape(shape + (2, CHAN // LANES, LANES)).transpose(0, 1, 3, 2, 4)
        return value.reshape(shape + (16, LANES))

    mine, tail = words(frames), words(tail_frames)
    bands = lax.axis_size("zl")
    following = lax.ppermute(mine[:, : TAPS - 1], "zl", [(b + 1, b) for b in range(bands - 1)])
    place = [lax.axis_index(axis) for axis in ("zl", "y", "zh")]
    my_x, my_core = lax.axis_index("x"), lax.axis_index("core")
    order = []
    for step in range(4):
        there = lax.rem(my_x + step, 4) * 2
        order += [there + my_core, there + 1 - my_core]
    place = jnp.stack(place + order).astype(jnp.int32)

    early = filter_transform(False, place, prototype, table, mine)
    late = filter_transform(True, place, prototype, table, mine, following, tail)

    exchange = functools.partial(
        lax.all_to_all, axis_name=("zh", "zl"), split_axis=0, concat_axis=0, tiled=True
    )
    recv, *late = lax.optimization_barrier((exchange(early[0]), *late))
    *halves, own = turn(place, recv)
    right0 = gather_x(own)
    first = [along_y(value, step) for value, step in zip(halves, (1, -1))]
    recv, last = lax.optimization_barrier((exchange(late[0]), late[1]))

    value, own = turn(place, recv)
    second = [along_y(value, -1)]
    right1 = [across_x(own)]

    value, own = turn(place, exchange(last))
    second.append(along_y(value, 1))
    right1.append(across_x(own))
    out = None
    for half in range(2):
        lefts, rights = (first[half], second[half]), (right0, right1[half])
        out = correlate(half, spectra, place, lefts, rights, out)
    return out


def solution(mesh):
    fine = Mesh(mesh.devices.reshape(4, 2, 4, 2, 4), ("x", "core", "y", "zh", "zl"))
    row_col = ("x", "core", "y", "zh")
    placed = (P(row_col, "zl", None, None), P(row_col, None, None, None), P())
    return jax.shard_map(
        shards,
        mesh=fine,
        in_specs=placed,
        out_specs=P(("x", "core"), ("y", "zh"), None, None, "zl"),
        check_vma=False,
    )
```
